128 devices in a mesh: row: 8 (over z, core), col: 16 (over x, y).
Axes of the slice: x: 4, y: 4, z: 4, core: 2. Of those that a mesh axis runs over, the one named last changes fastest.
Arguments:
- kernel: float32 [8, 8, 256, 4, 16, 256], P(None, 'row', None, None, 'col'), as said below
Outputs:
- factored: float32 [8, 8, 256, 4, 16, 256], P(None, 'row', None, None, 'col')
Inputs may be any that keep to these rules, and one draw needn't show every extreme that they name: kernel read as the 16384 by 16384 matrix is symmetric and positive definite, with every diagonal entry equal to 2 and every other entry in (0, 1].
All inputs are finite; a program needn't handle non-finite values.
Results may differ from the reference program's by a relative error of at most 0.0001.
Values sent between devices are 32-bit elements; how exact they have to be, the bound alone decides.
No kernel may reach another device: no remote copies, remote signals or barrier semaphores. Data moves between devices by JAX's collectives and lax.ppermute only.
A program may use at most 128 MiB of HBM per device.

```python
import jax
import jax.numpy as jnp
from jax import lax

NB = 256
TC = 4
GRID_ROWS = 8
GRID_COLS = 16
TR = 8


length_scale = 0.25


def draw_kernel(key, part):
    key = jax.random.fold_in(key, 7)
    full_order = NB * TC * GRID_COLS
    landmarks = jax.random.uniform(key, (full_order, 4), jnp.float32)
    distance = jnp.abs(landmarks[:, None, 0] - landmarks[None, :, 0])
    distance = distance + jnp.abs(landmarks[:, None, 1] - landmarks[None, :, 1])
    distance = distance + jnp.abs(landmarks[:, None, 2] - landmarks[None, :, 2])
    distance = distance + jnp.abs(landmarks[:, None, 3] - landmarks[None, :, 3])
    matrix = jnp.exp(-distance / length_scale) + jnp.eye(full_order, dtype=jnp.float32)
    return matrix.astype(jnp.float32).reshape(TR, GRID_ROWS, NB, TC, GRID_COLS, NB)


def setup_inputs(seed: int = 0) -> dict:
    splits = jax.random.split(jax.random.key(seed), 2)
    kernel = draw_kernel(jax.random.fold_in(splits[1], 71), 0)
    return {"kernel": kernel}


def reference(kernel):
    full_order = NB * TC * GRID_COLS
    matrix = kernel.reshape(full_order, full_order)
    for panel_index in range(2):
        lower_end = panel_index * NB
        upper_end = lower_end + NB
        pivot_factor = jnp.tril(jnp.linalg.cholesky(matrix[lower_end:upper_end, lower_end:upper_end]))
        below_panel = jax.scipy.linalg.solve_triangular(pivot_factor, matrix[upper_end:, lower_end:upper_end].T, lower=True).T
        trailing = matrix[upper_end:, upper_end:] - jnp.dot(below_panel, below_panel.T, precision=lax.Precision.HIGHEST)
        matrix = matrix.at[upper_end:, upper_end:].set(trailing)
        matrix = matrix.at[lower_end:upper_end, lower_end:upper_end].set(pivot_factor)
        matrix = matrix.at[upper_end:, lower_end:upper_end].set(below_panel)
        matrix = matrix.at[:lower_end, lower_end:upper_end].set(jnp.float32(0.0))
        matrix = matrix.at[lower_end:upper_end, upper_end:].set(jnp.float32(0.0))
    return matrix.reshape(TR, GRID_ROWS, NB, TC, GRID_COLS, NB)
```

```python
import jax
import jax.numpy as jnp
from jax import lax
from jax.experimental import pallas as pl
from jax.experimental.pallas import tpu as pltpu
from jax.sharding import PartitionSpec as P

F32 = jnp.float32
BF16 = jnp.bfloat16
ROWS, COLS = 8, 16
MIB = 1024 * 1024


def dot(a, b, ca, cb):
    return lax.dot_general(
        a,
        b,
        (((ca,), (cb,)), ((), ())),
        precision=lax.Precision.HIGHEST,
        preferred_element_type=F32,
    )


def matmul(a, b):
    return jnp.dot(a, b, preferred_element_type=F32)


def split(x):
    high = x.astype(BF16)
    return high, (x - high.astype(F32)).astype(BF16)


def prepare_kernel(x_ref, tile_ref, turned_ref):
    for m in range(4):
        for h in range(2):
            half = x_ref[pl.ds(2 * m + h, 256, stride=8), :]
            tile_ref[m, :, 128 * h : 128 * h + 128] = half
            turned_ref[m, 128 * h : 128 * h + 128, :] = half.T


def prepare(x):
    shape = jax.ShapeDtypeStruct((4, 256, 256), F32)
    return pl.pallas_call(
        prepare_kernel,
        grid=(1,),
        in_specs=[pl.BlockSpec((2048, 128), lambda i: (0, 0))],
        out_specs=[pl.BlockSpec((4, 256, 256), lambda i: (0, 0, 0))] * 2,
        out_shape=[shape, shape],
    )(x)


def inner(block):
    n = 16
    rows = [block[8 * j : 8 * j + 8, :] for j in range(n)]
    lane = lax.broadcasted_iota(jnp.int32, (8, 128), 1)
    sub = lax.broadcasted_iota(jnp.int32, (8, 128), 0)
    inv_rows = [jnp.where(lane == sub + 8 * j, 1.0, 0.0).astype(jnp.float32) for j in range(n)]
    full = lambda v: jnp.broadcast_to(v, (8, 128))
    us, ws = [], []
    for j in range(n):
        r, e = rows[j], inv_rows[j]
        cols = [full(r[:, 8 * j + c : 8 * j + c + 1]) for c in range(8)]
        a = [[full(cols[c][i : i + 1, :]) if i >= c else None for c in range(8)] for i in range(8)]
        l = [[None] * 8 for _ in range(8)]
        inv = [None] * 8
        for c in range(8):
            inv[c] = lax.rsqrt(a[c][c])
            for i in range(c + 1, 8):
                l[i][c] = a[i][c] * inv[c]
            for d in range(c + 1, 8):
                for i in range(d, 8):
                    a[i][d] = a[i][d] - l[i][c] * l[d][c]
        ru = [full(r[i : i + 1, :]) for i in range(8)]
        eu = [full(e[i : i + 1, :]) for i in range(8)]
        for c in range(8):
            ru[c] = ru[c] * inv[c]
            eu[c] = eu[c] * inv[c]
            for i in range(c + 1, 8):
                ru[i] = ru[i] - l[i][c] * ru[c]
                eu[i] = eu[i] - l[i][c] * eu[c]
        u, w = ru[0], eu[0]
        for c in range(1, 8):
            u = jnp.where(sub == c, ru[c], u)
            w = jnp.where(sub == c, eu[c], w)
        us.append(u)
        ws.append(w)
        for i in range(j + 1, n):
            ri, ei = rows[i], inv_rows[i]
            v = [full(ri[:, 8 * j + c : 8 * j + c + 1]) for c in range(8)]
            for c in range(8):
                v[c] = v[c] * inv[c]
                for d in range(c + 1, 8):
                    v[d] = v[d] - l[d][c] * v[c]
            for c in range(8):
                ri = ri - v[c] * ru[c]
                ei = ei - v[c] * eu[c]
            rows[i], inv_rows[i] = ri, ei
    return jnp.concatenate(us, axis=0), jnp.concatenate(ws, axis=0)

def factor_kernel(d_ref, lt_ref, w_ref, s):
    for j in range(16):
        for r in range(2):
            for c in range(2):
                s[256 * r + 16 * j : 256 * r + 16 * j + 16, 256 * c : 256 * c + 256] = d_ref[j, r, c]
    ri = lax.broadcasted_iota(jnp.int32, (512, 512), 0)
    ci = lax.broadcasted_iota(jnp.int32, (512, 512), 1)
    w_ref[...] = jnp.where(ri == ci, 1.0, 0.0).astype(F32)
    lane = lax.broadcasted_iota(jnp.int32, (128, 512), 1)
    r1 = lax.broadcasted_iota(jnp.int32, (128, 128), 0)
    c1 = lax.broadcasted_iota(jnp.int32, (128, 128), 1)

    @pl.loop(0, 4)
    def _(k):
        at = pl.multiple_of(k * 128, 128)
        u_kk, w_kk = inner(s[pl.ds(at, 128), pl.ds(at, 128)])
        u_kk = jnp.where(c1 >= r1, u_kk, 0.0)
        w_kk = jnp.where(c1 <= r1, w_kk, 0.0)
        u = dot(w_kk, s[pl.ds(at, 128), :], 1, 0)
        u = jnp.where(lane >= at + 128, u, 0.0)
        we = dot(w_kk, w_ref[pl.ds(at, 128), :], 1, 0)
        lt_ref[pl.ds(at, 128), :] = u
        lt_ref[pl.ds(at, 128), pl.ds(at, 128)] = u_kk
        s[...] -= dot(u, u, 0, 0)
        w_ref[...] -= dot(u, we, 0, 0)
        w_ref[pl.ds(at, 128), :] = we


def factor(d):
    shape = jax.ShapeDtypeStruct((512, 512), F32)
    return pl.pallas_call(
        factor_kernel,
        out_shape=[shape, shape],
        scratch_shapes=[pltpu.VMEM((512, 512), F32)],
        compiler_params=pltpu.CompilerParams(vmem_limit_bytes=16 * MIB),
        cost_estimate=pl.CostEstimate(flops=3 * 10**10, bytes_accessed=4 * MIB, transcendentals=0),
    )(d)


def update_kernel(
    place, x_ref, g0_ref, g1_ref, w_ref, lt_ref, mine_ref, other_ref, out_ref, wt3, bc3
):
    l = pl.program_id(0)
    row, col = place[0], place[1]

    @pl.when(l == 0)
    def _():
        w = w_ref[...]
        high, low = split(w.T)
        wt3[0:512, :] = high
        wt3[512:1024, :] = low
        high, low = split(w)
        is_first = lax.rem(row, 2) == 0
        for m in range(4):
            mine, other = mine_ref[m], other_ref[m]
            a0 = jnp.where(is_first, mine, other)
            a1 = jnp.where(is_first, other, mine)
            a0h, a0l = split(a0)
            a1h, a1l = split(a1)
            b0 = matmul(high[0:256, 0:256], a0h) + (
                matmul(high[0:256, 0:256], a0l) + matmul(low[0:256, 0:256], a0h)
            )
            ah = jnp.concatenate([a0h, a1h], axis=0)
            al = jnp.concatenate([a0l, a1l], axis=0)
            b1 = matmul(high[256:512], ah) + (matmul(high[256:512], al) + matmul(low[256:512], ah))
            bh, bl = split(jnp.concatenate([b0, b1], axis=0))
            bc3[0:512, 256 * m : 256 * m + 256] = bh
            bc3[512:1024, 256 * m : 256 * m + 256] = bl
            bc3[1024:1536, 256 * m : 256 * m + 256] = bh

    x0h, x0l = split(g0_ref[0])
    x1h, x1l = split(g1_ref[0])
    wh, wl = wt3[0:512, :], wt3[512:1024, :]
    b0 = matmul(x0h, wh[0:256, 0:256]) + (
        matmul(x0l, wh[0:256, 0:256]) + matmul(x0h, wl[0:256, 0:256])
    )
    xh = jnp.concatenate([x0h, x1h], axis=1)
    xl = jnp.concatenate([x0l, x1l], axis=1)
    b1 = matmul(xh, wh[:, 256:512]) + (matmul(xl, wh[:, 256:512]) + matmul(xh, wl[:, 256:512]))
    b = jnp.concatenate([b0, b1], axis=1)
    bh, bl = split(b)
    left = jnp.concatenate([bh, bh, bl], axis=1)
    for m in range(4):
        product = matmul(left, bc3[:, 256 * m : 256 * m + 256])
        for h in range(2):
            at = pl.ds(2 * m + h, 256, stride=8)
            out_ref[at, :] = x_ref[at, :] - product[:, 128 * h : 128 * h + 128]

    @pl.when(col <= 1)
    def _():
        for h in range(2):
            out_ref[pl.ds(h, 256, stride=8), :] = jnp.where(
                col == 0, b0[:, 128 * h : 128 * h + 128], b1[:, 128 * h : 128 * h + 128]
            )

    @pl.when((l == 0) & (row <= 1))
    def _():
        zero = jnp.zeros((256, 128), F32)
        for mh in range(2, 8):
            out_ref[pl.ds(mh, 256, stride=8), :] = zero
        first = lt_ref[0:256, 0:256].T
        second = lt_ref[256:512, 256:512].T
        for h in range(2):
            at = slice(128 * h, 128 * h + 128)
            value = jnp.where(
                row == 0,
                jnp.where(col == 0, first[:, at], zero),
                jnp.where(col == 0, b0[:, at], jnp.where(col == 1, second[:, at], zero)),
            )
            out_ref[pl.ds(h, 256, stride=8), :] = value


def position(row, l, k):
    q = 2 * (l // 2) + k
    x = (row // 4 + 2 * (l % 2) + q // 4) % 4
    y = (row % 4 + q % 4) % 4
    return 4 * x + y


def update(place, x, gathered, w, lt, mine, other):
    block = pl.BlockSpec((2048, 128), lambda l, place: (l, 0))
    whole = lambda *shape: pl.BlockSpec(shape, lambda l, place: (0,) * len(shape))
    return pl.pallas_call(
        update_kernel,
        grid_spec=pltpu.PrefetchScalarGridSpec(
            num_scalar_prefetch=1,
            grid=(8,),
            in_specs=[
                block,
                pl.BlockSpec((1, 256, 256), lambda l, place: (position(place[0], l, 0), 0, 0)),
                pl.BlockSpec((1, 256, 256), lambda l, place: (position(place[0], l, 1), 0, 0)),
                whole(512, 512),
                whole(512, 512),
                whole(4, 256, 256),
                whole(4, 256, 256),
            ],
            out_specs=block,
            scratch_shapes=[pltpu.VMEM((1024, 512), BF16), pltpu.VMEM((1536, 1024), BF16)],
        ),
        out_shape=jax.ShapeDtypeStruct((16384, 128), F32),
        compiler_params=pltpu.CompilerParams(vmem_limit_bytes=48 * MIB),
    )(place, x, gathered, gathered, w, lt, mine, other)


def scatter_pairs(m):
    pairs = []
    for k in range(2):
        for c in range(COLS):
            row = c % ROWS
            target = position(row, 2 * m + c // ROWS, k)
            pairs.append((k * COLS + c, row * COLS + target))
    return pairs


def shards(kernel):
    row, col = lax.axis_index("row"), lax.axis_index("col")
    x = kernel.reshape(16384, 128)
    tile, turned = prepare(x)

    both = ("row", "col")
    share = sum(lax.ppermute(turned[m], both, scatter_pairs(m)) for m in range(4))
    gathered = lax.all_gather(share, "col")

    came = [
        lax.ppermute(tile, "row", [(k, 2 * z + k) for k in range(2)]) for z in (1, 3, 2)
    ]
    d = lax.all_to_all(tile[0].reshape(16, 16, 256), "col", 0, 0, tiled=True)[0:2]
    d = jnp.broadcast_to(d[None], (8, 2, 16, 256))
    d = lax.all_to_all(d, "row", 0, 0, tiled=True)[0:2]
    d = jnp.broadcast_to(d[None], (16, 2, 2, 16, 256))
    d = lax.all_to_all(d, "col", 0, 0, tiled=True)
    lt, w = factor(d)

    came, lt, w = lax.optimization_barrier((came, lt, w))
    mine = jnp.where(row < 2, tile, sum(came))
    other = lax.ppermute(mine, "row", [(r, r ^ 1) for r in range(ROWS)])
    place = jnp.stack([row, col]).astype(jnp.int32)
    return update(place, x, gathered, w, lt, mine, other).reshape(kernel.shape)


def solution(mesh):
    placed = P(None, "row", None, None, "col", None)
    return jax.shard_map(
        shards, mesh=mesh, in_specs=(placed,), out_specs=placed, check_vma=False
    )
```

```python
import jax
import jax.numpy as jnp
from jax import lax
from jax.experimental import pallas as pl
from jax.experimental.pallas import tpu as pltpu
from jax.sharding import PartitionSpec as P

F32 = jnp.float32
BF16 = jnp.bfloat16
ROWS, COLS = 8, 16
MIB = 1024 * 1024


def dot(a, b, ca, cb):
    return lax.dot_general(
        a,
        b,
        (((ca,), (cb,)), ((), ())),
        precision=lax.Precision.HIGHEST,
        preferred_element_type=F32,
    )


def matmul(a, b):
    return jnp.dot(a, b, preferred_element_type=F32)


def split(x):
    high = x.astype(BF16)
    return high, (x - high.astype(F32)).astype(BF16)


def prepare_kernel(x_ref, tile_ref, tiles_ref, *rest):
    turned_refs, (rows, done) = rest[:4], rest[4:]
    copy = pltpu.make_async_copy(x_ref.at[0:2048], rows, done)
    copy.start()
    copy.wait()
    for m in range(4):
        for h in range(2):
            half = rows[pl.ds(2 * m + h, 256, stride=8), :]
            if m == 0:
                tile_ref[:, 128 * h : 128 * h + 128] = half
            tiles_ref[m, :, 128 * h : 128 * h + 128] = half
            turned_refs[m][128 * h : 128 * h + 128, :] = half.T


def prepare(x):
    vmem = pl.BlockSpec(memory_space=pltpu.VMEM)
    square = jax.ShapeDtypeStruct((256, 256), F32)
    return pl.pallas_call(
        prepare_kernel,
        in_specs=[pl.BlockSpec(memory_space=pl.ANY)],
        out_specs=[vmem] * 6,
        out_shape=[square, jax.ShapeDtypeStruct((4, 256, 256), F32)] + [square] * 4,
        scratch_shapes=[pltpu.VMEM((2048, 128), F32), pltpu.SemaphoreType.DMA],
        compiler_params=pltpu.CompilerParams(vmem_limit_bytes=58 * MIB),
    )(x)


def inner(block):
    n = 16
    rows = [block[8 * j : 8 * j + 8, :] for j in range(n)]
    lane = lax.broadcasted_iota(jnp.int32, (8, 128), 1)
    sub = lax.broadcasted_iota(jnp.int32, (8, 128), 0)
    inv_rows = [jnp.where(lane == sub + 8 * j, 1.0, 0.0).astype(jnp.float32) for j in range(n)]
    full = lambda v: jnp.broadcast_to(v, (8, 128))
    us, ws = [], []
    for j in range(n):
        r, e = rows[j], inv_rows[j]
        cols = [full(r[:, 8 * j + c : 8 * j + c + 1]) for c in range(8)]
        a = [[full(cols[c][i : i + 1, :]) if i >= c else None for c in range(8)] for i in range(8)]
        l = [[None] * 8 for _ in range(8)]
        inv = [None] * 8
        for c in range(8):
            inv[c] = lax.rsqrt(a[c][c])
            for i in range(c + 1, 8):
                l[i][c] = a[i][c] * inv[c]
            for d in range(c + 1, 8):
                for i in range(d, 8):
                    a[i][d] = a[i][d] - l[i][c] * l[d][c]
        ru = [full(r[i : i + 1, :]) for i in range(8)]
        eu = [full(e[i : i + 1, :]) for i in range(8)]
        for c in range(8):
            ru[c] = ru[c] * inv[c]
            eu[c] = eu[c] * inv[c]
            for i in range(c + 1, 8):
                ru[i] = ru[i] - l[i][c] * ru[c]
                eu[i] = eu[i] - l[i][c] * eu[c]
        u, w = ru[0], eu[0]
        for c in range(1, 8):
            u = jnp.where(sub == c, ru[c], u)
            w = jnp.where(sub == c, eu[c], w)
        us.append(u)
        ws.append(w)
        for i in range(j + 1, n):
            ri, ei = rows[i], inv_rows[i]
            v = [full(ri[:, 8 * j + c : 8 * j + c + 1]) for c in range(8)]
            for c in range(8):
                v[c] = v[c] * inv[c]
                for d in range(c + 1, 8):
                    v[d] = v[d] - l[d][c] * v[c]
            for c in range(8):
                ri = ri - v[c] * ru[c]
                ei = ei - v[c] * eu[c]
            rows[i], inv_rows[i] = ri, ei
    return jnp.concatenate(us, axis=0), jnp.concatenate(ws, axis=0)

def factor_256(s, lt_ref, w_ref, diag):
    r1 = lax.broadcasted_iota(jnp.int32, (128, 128), 0)
    c1 = lax.broadcasted_iota(jnp.int32, (128, 128), 1)
    right = s[0:128, 128:256]
    diag[0] = s[0:128, 0:128]
    diag[1] = s[128:256, 128:256]
    lt_ref[128:256, 0:128] = jnp.zeros((128, 128), F32)
    w_ref[0:128, 128:256] = jnp.zeros((128, 128), F32)

    @pl.loop(0, 2)
    def _(k):
        at = pl.multiple_of(k * 128, 128)
        u, w = inner(diag[k])
        w = jnp.where(c1 <= r1, w, 0.0)
        lt_ref[pl.ds(at, 128), pl.ds(at, 128)] = jnp.where(c1 >= r1, u, 0.0)
        w_ref[pl.ds(at, 128), pl.ds(at, 128)] = w

        @pl.when(k == 0)
        def _():
            u01 = dot(w, right, 1, 0)
            lt_ref[0:128, 128:256] = u01
            diag[1] -= dot(u01, u01, 0, 0)

    under = dot(lt_ref[0:128, 128:256], w_ref[0:128, 0:128], 0, 0)
    w_ref[128:256, 0:128] = -dot(w_ref[128:256, 128:256], under, 1, 0)


def factor_kernel(d_ref, *rest):
    lt0_ref, lt1_ref, w0_ref, w1_ref, under_ref, s, right, diag = rest
    for j in range(16):
        at = slice(16 * j, 16 * j + 16)
        s[at, :] = d_ref[j, 0]
    factor_256(s, lt0_ref, w0_ref, diag)
    for j in range(16):
        at = slice(16 * j, 16 * j + 16)
        right[at, :] = d_ref[j, 1]
        s[at, :] = d_ref[j, 2]
    u = dot(w0_ref[...], right[...], 1, 0)
    s[...] -= dot(u, u, 0, 0)
    factor_256(s, lt1_ref, w1_ref, diag)
    under_ref[...] = -dot(w1_ref[...], dot(u, w0_ref[...], 0, 0), 1, 0)


def factor(d):
    square = jax.ShapeDtypeStruct((256, 256), F32)
    return pl.pallas_call(
        factor_kernel,
        out_shape=[square] * 5,
        scratch_shapes=[pltpu.VMEM((256, 256), F32)] * 2 + [pltpu.VMEM((2, 128, 128), F32)],
        compiler_params=pltpu.CompilerParams(vmem_limit_bytes=16 * MIB),
        cost_estimate=pl.CostEstimate(flops=0, bytes_accessed=0, transcendentals=0),
    )(d)


def update_kernel(
    place, x_ref, g_ref, w0_ref, w1_ref, under_ref, lt0_ref, lt1_ref, mine_ref, other_ref, out_ref,
    old, new, tiles, wt, bc, old_sem, new_sem, tile_sem,
):
    row, col = place[0], place[1]

    def load(l, mh):
        at = pl.ds(l * 256, 256)
        return pltpu.make_async_copy(
            x_ref.at[at, mh], old.at[l, :, pl.ds(128 * mh, 128)], old_sem.at[l, mh]
        )

    def fetch(l, k):
        return pltpu.make_async_copy(
            g_ref.at[position(row, l, k)], tiles.at[l, k], tile_sem.at[l, k]
        )

    def store(l, mh):
        at = pl.ds(l * 256, 256)
        return pltpu.make_async_copy(
            new.at[l % 2, :, pl.ds(128 * mh, 128)], out_ref.at[at, mh], new_sem.at[l % 2, mh]
        )

    @pl.loop(0, 8)
    def _(l):
        for k in range(2):
            fetch(l, k).start()
        for mh in range(8):
            load(l, mh).start()

    w = jnp.concatenate(
        [
            jnp.concatenate([w0_ref[...], jnp.zeros((256, 256), F32)], axis=1),
            jnp.concatenate([under_ref[...], w1_ref[...]], axis=1),
        ],
        axis=0,
    )
    high, low = split(w.T)
    wt[0:512, :] = high
    wt[512:1024, :] = low
    high, low = split(w)
    is_first = lax.rem(row, 2) == 0
    for m in range(4):
        mine, other = mine_ref[m], other_ref[m]
        a0h, a0l = split(jnp.where(is_first, mine, other))
        a1h, a1l = split(jnp.where(is_first, other, mine))
        b0 = matmul(high[0:256, 0:256], a0h) + (
            matmul(high[0:256, 0:256], a0l) + matmul(low[0:256, 0:256], a0h)
        )
        ah = jnp.concatenate([a0h, a1h], axis=0)
        al = jnp.concatenate([a0l, a1l], axis=0)
        b1 = matmul(high[256:512], ah) + (matmul(high[256:512], al) + matmul(low[256:512], ah))
        bh, bl = split(jnp.concatenate([b0, b1], axis=0))
        bc[0:512, 256 * m : 256 * m + 256] = bh
        bc[512:1024, 256 * m : 256 * m + 256] = bl
        bc[1024:1536, 256 * m : 256 * m + 256] = bh

    @pl.loop(0, 8)
    def _(l):
        for k in range(2):
            fetch(l, k).wait()
        x0h, x0l = split(tiles[l, 0])
        x1h, x1l = split(tiles[l, 1])
        wh, wl = wt[0:512, :], wt[512:1024, :]
        b0 = matmul(x0h, wh[0:256, 0:256]) + (
            matmul(x0l, wh[0:256, 0:256]) + matmul(x0h, wl[0:256, 0:256])
        )
        xh = jnp.concatenate([x0h, x1h], axis=1)
        xl = jnp.concatenate([x0l, x1l], axis=1)
        b1 = matmul(xh, wh[:, 256:512]) + (
            matmul(xl, wh[:, 256:512]) + matmul(xh, wl[:, 256:512])
        )
        bh, bl = split(jnp.concatenate([b0, b1], axis=1))
        left = jnp.concatenate([bh, bh, bl], axis=1)

        for mh in range(8):
            load(l, mh).wait()

        @pl.when(l >= 2)
        def _():
            for mh in range(8):
                store(l - 2, mh).wait()

        slot = l % 2
        for m in range(4):
            at = slice(256 * m, 256 * m + 256)
            new[slot, :, at] = old[l, :, at] - matmul(left, bc[:, at])

        @pl.when(col <= 1)
        def _():
            new[slot, :, 0:256] = jnp.where(col == 0, b0, b1)

        @pl.when((l == 0) & (row <= 1))
        def _():
            zero = jnp.zeros((256, 256), F32)
            new[slot, :, 256:1024] = jnp.zeros((256, 768), F32)
            new[slot, :, 0:256] = jnp.where(
                row == 0,
                jnp.where(col == 0, lt0_ref[...].T, zero),
                jnp.where(col == 0, b0, jnp.where(col == 1, lt1_ref[...].T, zero)),
            )

        for mh in range(8):
            store(l, mh).start()

    for l in (6, 7):
        for mh in range(8):
            store(l, mh).wait()


def position(row, l, k):
    q = 2 * (l // 2) + k
    x = (row // 4 + 2 * (l % 2) + q // 4) % 4
    y = (row % 4 + q % 4) % 4
    return 4 * x + y


def update(place, x, gathered, w0, w1, under, lt0, lt1, mine, other):
    vmem = pl.BlockSpec(memory_space=pltpu.VMEM)
    hbm = pl.BlockSpec(memory_space=pl.ANY)
    return pl.pallas_call(
        update_kernel,
        in_specs=[pl.BlockSpec(memory_space=pltpu.SMEM), hbm, hbm] + [vmem] * 7,
        out_specs=hbm,
        out_shape=jax.ShapeDtypeStruct((2048, 8, 128), F32),
        scratch_shapes=[
            pltpu.VMEM((8, 256, 1024), F32),
            pltpu.VMEM((2, 256, 1024), F32),
            pltpu.VMEM((8, 2, 256, 256), F32),
            pltpu.VMEM((1024, 512), BF16),
            pltpu.VMEM((1536, 1024), BF16),
            pltpu.SemaphoreType.DMA((8, 8)),
            pltpu.SemaphoreType.DMA((2, 8)),
            pltpu.SemaphoreType.DMA((8, 2)),
        ],
        compiler_params=pltpu.CompilerParams(vmem_limit_bytes=48 * MIB),
    )(place, x, gathered, w0, w1, under, lt0, lt1, mine, other)


def scatter_pairs(m):
    pairs = []
    for k in range(2):
        for c in range(COLS):
            row = c % ROWS
            target = position(row, 2 * m + c // ROWS, k)
            pairs.append((k * COLS + c, row * COLS + target))
    return pairs


def along_z(array, step):
    return lax.ppermute(array, "row", [(k, 2 * step + k) for k in range(2)])


def shards(kernel):
    row, col = lax.axis_index("row"), lax.axis_index("col")
    place = jnp.stack([row, col]).astype(jnp.int32)
    x = kernel.reshape(16384, 128)
    tile, tiles, *turned = prepare(x)

    pieces = [lax.ppermute(turned[m], ("row", "col"), scatter_pairs(m)) for m in range(4)]
    d = lax.all_to_all(tile.reshape(16, 16, 256), "col", 0, 0, tiled=True)[0:2]
    pieces, d = lax.optimization_barrier((pieces, d))
    share = sum(pieces)
    share, d = lax.optimization_barrier((share, d))
    gathered = lax.all_gather(share, "col")

    d = lax.all_to_all(jnp.broadcast_to(d[None], (8, 2, 16, 256)), "row", 0, 0, tiled=True)
    d = jnp.stack([d[0, 0], d[0, 1], d[1, 1]])
    tiles, d = lax.optimization_barrier((tiles, d))
    came = [along_z(tiles, step) for step in (1, 3, 2)]
    d = lax.all_to_all(jnp.broadcast_to(d[None], (16, 3, 16, 256)), "col", 0, 0, tiled=True)
    lt0, lt1, w0, w1, under = factor(d)

    came, w1 = lax.optimization_barrier((came, w1))
    mine = jnp.where(row < 2, tiles, sum(came))
    other = lax.ppermute(mine, "row", [(r, r ^ 1) for r in range(ROWS)])
    cells = kernel.reshape(2048, 8, 128)
    out = update(place, cells, gathered, w0, w1, under, lt0, lt1, mine, other)
    return out.reshape(kernel.shape)


def solution(mesh):
    placed = P(None, "row", None, None, "col", None)
    return jax.shard_map(
        shards, mesh=mesh, in_specs=(placed,), out_specs=placed, check_vma=False
    )
```

```python
import jax
import jax.numpy as jnp
from jax import lax
from jax.experimental import pallas as pl
from jax.experimental.pallas import tpu as pltpu
from jax.sharding import PartitionSpec as P

F32 = jnp.float32
BF16 = jnp.bfloat16
ROWS, COLS = 8, 16
MIB = 1024 * 1024


def dot(a, b, ca, cb):
    return lax.dot_general(
        a,
        b,
        (((ca,), (cb,)), ((), ())),
        precision=lax.Precision.HIGHEST,
        preferred_element_type=F32,
    )


def matmul(a, b):
    return jnp.dot(a, b, preferred_element_type=F32)


def split(x):
    high = x.astype(BF16)
    return high, (x - high.astype(F32)).astype(BF16)


def prepare_kernel(x_ref, tile_ref, tiles_ref, *rest):
    turned_refs, (rows, done) = rest[:4], rest[4:]
    copy = pltpu.make_async_copy(x_ref.at[0:2048], rows, done)
    copy.start()
    copy.wait()
    for m in range(4):
        for h in range(2):
            half = rows[pl.ds(2 * m + h, 256, stride=8), :]
            if m == 0:
                tile_ref[:, 128 * h : 128 * h + 128] = half
            tiles_ref[m, :, 128 * h : 128 * h + 128] = half
            turned_refs[m][128 * h : 128 * h + 128, :] = half.T


def prepare(x):
    vmem = pl.BlockSpec(memory_space=pltpu.VMEM)
    square = jax.ShapeDtypeStruct((256, 256), F32)
    return pl.pallas_call(
        prepare_kernel,
        in_specs=[pl.BlockSpec(memory_space=pl.ANY)],
        out_specs=[vmem] * 6,
        out_shape=[square, jax.ShapeDtypeStruct((4, 256, 256), F32)] + [square] * 4,
        scratch_shapes=[pltpu.VMEM((2048, 128), F32), pltpu.SemaphoreType.DMA],
        compiler_params=pltpu.CompilerParams(vmem_limit_bytes=58 * MIB),
    )(x)


def inner(block):
    n = 16
    rows = [block[8 * j : 8 * j + 8, :] for j in range(n)]
    lane = lax.broadcasted_iota(jnp.int32, (8, 128), 1)
    sub = lax.broadcasted_iota(jnp.int32, (8, 128), 0)
    inv_rows = [jnp.where(lane == sub + 8 * j, 1.0, 0.0).astype(jnp.float32) for j in range(n)]
    full = lambda v: jnp.broadcast_to(v, (8, 128))
    us, ws = [], []
    for j in range(n):
        r, e = rows[j], inv_rows[j]
        cols = [full(r[:, 8 * j + c : 8 * j + c + 1]) for c in range(8)]
        a = [[full(cols[c][i : i + 1, :]) if i >= c else None for c in range(8)] for i in range(8)]
        l = [[None] * 8 for _ in range(8)]
        inv = [None] * 8
        for c in range(8):
            inv[c] = lax.rsqrt(a[c][c])
            for i in range(c + 1, 8):
                l[i][c] = a[i][c] * inv[c]
            for d in range(c + 1, 8):
                for i in range(d, 8):
                    a[i][d] = a[i][d] - l[i][c] * l[d][c]
        ru = [full(r[i : i + 1, :]) for i in range(8)]
        eu = [full(e[i : i + 1, :]) for i in range(8)]
        for c in range(8):
            ru[c] = ru[c] * inv[c]
            eu[c] = eu[c] * inv[c]
            for i in range(c + 1, 8):
                ru[i] = ru[i] - l[i][c] * ru[c]
                eu[i] = eu[i] - l[i][c] * eu[c]
        u, w = ru[0], eu[0]
        for c in range(1, 8):
            u = jnp.where(sub == c, ru[c], u)
            w = jnp.where(sub == c, eu[c], w)
        us.append(u)
        ws.append(w)
        for i in range(j + 1, n):
            ri, ei = rows[i], inv_rows[i]
            v = [full(ri[:, 8 * j + c : 8 * j + c + 1]) for c in range(8)]
            for c in range(8):
                v[c] = v[c] * inv[c]
                for d in range(c + 1, 8):
                    v[d] = v[d] - l[d][c] * v[c]
            for c in range(8):
                ri = ri - v[c] * ru[c]
                ei = ei - v[c] * eu[c]
            rows[i], inv_rows[i] = ri, ei
    return jnp.concatenate(us, axis=0), jnp.concatenate(ws, axis=0)

def factor_256(s, lt_ref, w_ref, diag):
    r1 = lax.broadcasted_iota(jnp.int32, (128, 128), 0)
    c1 = lax.broadcasted_iota(jnp.int32, (128, 128), 1)
    right = s[0:128, 128:256]
    diag[0] = s[0:128, 0:128]
    diag[1] = s[128:256, 128:256]
    lt_ref[128:256, 0:128] = jnp.zeros((128, 128), F32)
    w_ref[0:128, 128:256] = jnp.zeros((128, 128), F32)

    @pl.loop(0, 2)
    def _(k):
        at = pl.multiple_of(k * 128, 128)
        u, w = inner(diag[k])
        w = jnp.where(c1 <= r1, w, 0.0)
        lt_ref[pl.ds(at, 128), pl.ds(at, 128)] = jnp.where(c1 >= r1, u, 0.0)
        w_ref[pl.ds(at, 128), pl.ds(at, 128)] = w

        @pl.when(k == 0)
        def _():
            u01 = dot(w, right, 1, 0)
            lt_ref[0:128, 128:256] = u01
            diag[1] -= dot(u01, u01, 0, 0)

    under = dot(lt_ref[0:128, 128:256], w_ref[0:128, 0:128], 0, 0)
    w_ref[128:256, 0:128] = -dot(w_ref[128:256, 128:256], under, 1, 0)


def factor_kernel(d_ref, *rest):
    lt0_ref, lt1_ref, w0_ref, w1_ref, under_ref, s, right, diag = rest
    for j in range(16):
        at = slice(16 * j, 16 * j + 16)
        s[at, :] = d_ref[j, 0]
    factor_256(s, lt0_ref, w0_ref, diag)
    for j in range(16):
        at = slice(16 * j, 16 * j + 16)
        right[at, :] = d_ref[j, 1]
        s[at, :] = d_ref[j, 2]
    u = dot(w0_ref[...], right[...], 1, 0)
    s[...] -= dot(u, u, 0, 0)
    factor_256(s, lt1_ref, w1_ref, diag)
    under_ref[...] = -dot(w1_ref[...], dot(u, w0_ref[...], 0, 0), 1, 0)


def factor(d):
    square = jax.ShapeDtypeStruct((256, 256), F32)
    return pl.pallas_call(
        factor_kernel,
        out_shape=[square] * 5,
        scratch_shapes=[pltpu.VMEM((256, 256), F32)] * 2 + [pltpu.VMEM((2, 128, 128), F32)],
        compiler_params=pltpu.CompilerParams(vmem_limit_bytes=16 * MIB),
        cost_estimate=pl.CostEstimate(flops=0, bytes_accessed=0, transcendentals=0),
    )(d)


def product(a, b):
    return matmul(a[0], b[0]) + (matmul(a[0], b[1]) + matmul(a[1], b[0]))


def columns(is_first, w0_ref, w1_ref, under_ref, column, wt_ref, z_ref):
    w = jnp.concatenate(
        [
            jnp.concatenate([w0_ref[...], jnp.zeros((256, 256), F32)], axis=1),
            jnp.concatenate([under_ref[...], w1_ref[...]], axis=1),
        ],
        axis=0,
    )
    turned = split(w.T)
    wt_ref[0:512, :] = turned[0]
    wt_ref[512:1024, :] = turned[1]
    w = split(w)
    for m in range(4):
        at = slice(256 * m, 256 * m + 256)
        mine, other = column(m)
        a0 = jnp.where(is_first, mine, other)
        a1 = jnp.where(is_first, other, mine)
        b0 = product([p[0:256, 0:256] for p in w], split(a0))
        b1 = product([p[256:512] for p in w], split(jnp.concatenate([a0, a1], axis=0)))
        b0, b1 = split(b0), split(b1)
        z0 = product([p[0:256] for p in turned], [jnp.concatenate(p, axis=0) for p in zip(b0, b1)])
        z1 = product([p[256:512, 256:512] for p in turned], b1)
        zh, zl = split(jnp.concatenate([z0, z1], axis=0))
        z_ref[0:512, at] = zh
        z_ref[512:1024, at] = zl
        z_ref[1024:1536, at] = zh


def update_kernel(
    place, x_ref, g_ref, w0_ref, w1_ref, under_ref, lt0_ref, lt1_ref, mine_ref, other_ref, out_ref,
    old, new, tiles, wt, z, near, old_sem, new_sem, tile_sem, near_sem,
):
    row, col = place[0], place[1]

    def load(l, mh):
        at = pl.ds(l * 256, 256)
        return pltpu.make_async_copy(
            x_ref.at[at, mh], old.at[l, :, pl.ds(128 * mh, 128)], old_sem.at[l, mh]
        )

    def fetch(l, k):
        return pltpu.make_async_copy(
            g_ref.at[position(row, l, k)], tiles.at[l, k], tile_sem.at[l, k]
        )

    def store(l, mh):
        at = pl.ds(l * 256, 256)
        return pltpu.make_async_copy(
            new.at[l % 2, :, pl.ds(128 * mh, 128)], out_ref.at[at, mh], new_sem.at[l % 2, mh]
        )

    def take(i, m):
        source = (mine_ref, other_ref)[i]
        return pltpu.make_async_copy(source.at[m], near.at[i, m], near_sem.at[i, m])

    for m in range(4):
        for i in range(2):
            take(i, m).start()

    @pl.loop(0, 8)
    def _(l):
        for k in range(2):
            fetch(l, k).start()
        for mh in range(8):
            load(l, mh).start()

    def column(m):
        for i in range(2):
            take(i, m).wait()
        return near[0, m], near[1, m]

    columns(lax.rem(row, 2) == 0, w0_ref, w1_ref, under_ref, column, wt, z)

    @pl.loop(0, 8)
    def _(l):
        for k in range(2):
            fetch(l, k).wait()
        xh, xl = split(jnp.concatenate([tiles[l, 0], tiles[l, 1]], axis=1))
        left = jnp.concatenate([xh, xh, xl], axis=1)

        for mh in range(8):
            load(l, mh).wait()

        @pl.when(l >= 2)
        def _():
            for mh in range(8):
                store(l - 2, mh).wait()

        slot = l % 2
        for m in range(1, 4):
            at = slice(256 * m, 256 * m + 256)
            new[slot, :, at] = old[l, :, at] - matmul(left, z[:, at])

        @pl.when(col > 1)
        def _():
            new[slot, :, 0:256] = old[l, :, 0:256] - matmul(left, z[:, 0:256])

        @pl.when(col == 0)
        def _():
            x = (xh[:, 0:256], xl[:, 0:256])
            new[slot, :, 0:256] = product(x, (wt[0:256, 0:256], wt[512:768, 0:256]))

        @pl.when(col == 1)
        def _():
            new[slot, :, 0:256] = product((xh, xl), (wt[0:512, 256:512], wt[512:1024, 256:512]))

        @pl.when((l == 0) & (row <= 1))
        def _():
            new[slot, :, 256:1024] = jnp.zeros((256, 768), F32)

            @pl.when((row == 0) | (col > 0))
            def _():
                own = jnp.where(row == 0, lt0_ref[...].T, lt1_ref[...].T)
                new[slot, :, 0:256] = jnp.where(col == row, own, 0.0)

        for mh in range(8):
            store(l, mh).start()

    for l in (6, 7):
        for mh in range(8):
            store(l, mh).wait()


def position(row, l, k):
    q = 2 * (l // 2) + k
    x = (row // 4 + 2 * (l % 2) + q // 4) % 4
    y = (row % 4 + q % 4) % 4
    return 4 * x + y


def update(place, x, gathered, w0, w1, under, lt0, lt1, mine, other):
    vmem = pl.BlockSpec(memory_space=pltpu.VMEM)
    hbm = pl.BlockSpec(memory_space=pl.ANY)
    return pl.pallas_call(
        update_kernel,
        in_specs=[pl.BlockSpec(memory_space=pltpu.SMEM), hbm, hbm] + [vmem] * 5 + [hbm] * 2,
        out_specs=hbm,
        out_shape=jax.ShapeDtypeStruct((2048, 8, 128), F32),
        scratch_shapes=[
            pltpu.VMEM((8, 256, 1024), F32),
            pltpu.VMEM((2, 256, 1024), F32),
            pltpu.VMEM((8, 2, 256, 256), F32),
            pltpu.VMEM((1024, 512), BF16),
            pltpu.VMEM((1536, 1024), BF16),
            pltpu.VMEM((2, 4, 256, 256), F32),
            pltpu.SemaphoreType.DMA((8, 8)),
            pltpu.SemaphoreType.DMA((2, 8)),
            pltpu.SemaphoreType.DMA((8, 2)),
            pltpu.SemaphoreType.DMA((2, 4)),
        ],
        compiler_params=pltpu.CompilerParams(vmem_limit_bytes=48 * MIB),
    )(place, x, gathered, w0, w1, under, lt0, lt1, mine, other)


def scatter_pairs(m):
    pairs = []
    for k in range(2):
        for c in range(COLS):
            row = c % ROWS
            target = position(row, 2 * m + c // ROWS, k)
            pairs.append((k * COLS + c, row * COLS + target))
    return pairs


def along_z(array, step):
    return lax.ppermute(array, "row", [(k, 2 * step + k) for k in range(2)])


def shards(kernel):
    row, col = lax.axis_index("row"), lax.axis_index("col")
    place = jnp.stack([row, col]).astype(jnp.int32)
    x = kernel.reshape(16384, 128)
    tile, tiles, *turned = prepare(x)

    pieces = [lax.ppermute(turned[m], ("row", "col"), scatter_pairs(m)) for m in range(4)]
    d = lax.all_to_all(tile.reshape(16, 16, 256), "col", 0, 0, tiled=True)[0:2]
    pieces, d = lax.optimization_barrier((pieces, d))
    share = sum(pieces)
    share, d = lax.optimization_barrier((share, d))
    gathered = lax.all_gather(share, "col")

    d = lax.all_to_all(jnp.broadcast_to(d[None], (8, 2, 16, 256)), "row", 0, 0, tiled=True)
    d = jnp.stack([d[0, 0], d[0, 1], d[1, 1]])
    tiles, d = lax.optimization_barrier((tiles, d))
    came = [along_z(tiles, step) for step in (1, 3, 2)]
    d = lax.all_to_all(jnp.broadcast_to(d[None], (16, 3, 16, 256)), "col", 0, 0, tiled=True)
    lt0, lt1, w0, w1, under = factor(d)

    came, w1 = lax.optimization_barrier((came, w1))
    mine = jnp.where(row < 2, tiles, sum(came))
    other = lax.ppermute(mine, "row", [(r, r ^ 1) for r in range(ROWS)])
    cells = kernel.reshape(2048, 8, 128)
    out = update(place, cells, gathered, w0, w1, under, lt0, lt1, mine, other)
    return out.reshape(kernel.shape)


def solution(mesh):
    placed = P(None, "row", None, None, "col", None)
    return jax.shard_map(
        shards, mesh=mesh, in_specs=(placed,), out_specs=placed, check_vma=False
    )
```

```python
import jax
import jax.numpy as jnp
from jax import lax
from jax.experimental import pallas as pl
from jax.experimental.pallas import tpu as pltpu
from jax.sharding import PartitionSpec as P

F32 = jnp.float32
BF16 = jnp.bfloat16
ROWS, COLS = 8, 16
MIB = 1024 * 1024


def dot(a, b, ca, cb):
    return lax.dot_general(
        a,
        b,
        (((ca,), (cb,)), ((), ())),
        precision=lax.Precision.HIGHEST,
        preferred_element_type=F32,
    )


def matmul(a, b):
    return jnp.dot(a, b, preferred_element_type=F32)


def split(x):
    high = x.astype(BF16)
    return high, (x - high.astype(F32)).astype(BF16)


def prepare_kernel(x_ref, tile_ref, tiles_ref, *rest):
    turned_refs, (rows, done) = rest[:4], rest[4:]
    copy = pltpu.make_async_copy(x_ref.at[0:2048], rows, done)
    copy.start()
    copy.wait()
    for m in range(4):
        for h in range(2):
            half = rows[pl.ds(2 * m + h, 256, stride=8), :]
            if m == 0:
                tile_ref[:, 128 * h : 128 * h + 128] = half
            tiles_ref[m, :, 128 * h : 128 * h + 128] = half
            turned_refs[m][128 * h : 128 * h + 128, :] = half.T


def prepare(x):
    vmem = pl.BlockSpec(memory_space=pltpu.VMEM)
    square = jax.ShapeDtypeStruct((256, 256), F32)
    return pl.pallas_call(
        prepare_kernel,
        in_specs=[pl.BlockSpec(memory_space=pl.ANY)],
        out_specs=[vmem] * 6,
        out_shape=[square, jax.ShapeDtypeStruct((4, 256, 256), F32)] + [square] * 4,
        scratch_shapes=[pltpu.VMEM((2048, 128), F32), pltpu.SemaphoreType.DMA],
        compiler_params=pltpu.CompilerParams(vmem_limit_bytes=58 * MIB),
    )(x)


def inner(block):
    n = 16
    rows = [block[8 * j : 8 * j + 8, :] for j in range(n)]
    lane = lax.broadcasted_iota(jnp.int32, (8, 128), 1)
    sub = lax.broadcasted_iota(jnp.int32, (8, 128), 0)
    inv_rows = [jnp.where(lane == sub + 8 * j, 1.0, 0.0).astype(jnp.float32) for j in range(n)]
    full = lambda v: jnp.broadcast_to(v, (8, 128))
    us, ws = [], []
    for j in range(n):
        r, e = rows[j], inv_rows[j]
        cols = [full(r[:, 8 * j + c : 8 * j + c + 1]) for c in range(8)]
        a = [[full(cols[c][i : i + 1, :]) if i >= c else None for c in range(8)] for i in range(8)]
        l = [[None] * 8 for _ in range(8)]
        inv = [None] * 8
        for c in range(8):
            inv[c] = lax.rsqrt(a[c][c])
            for i in range(c + 1, 8):
                l[i][c] = a[i][c] * inv[c]
            for d in range(c + 1, 8):
                for i in range(d, 8):
                    a[i][d] = a[i][d] - l[i][c] * l[d][c]
        ru = [full(r[i : i + 1, :]) for i in range(8)]
        eu = [full(e[i : i + 1, :]) for i in range(8)]
        for c in range(8):
            ru[c] = ru[c] * inv[c]
            eu[c] = eu[c] * inv[c]
            for i in range(c + 1, 8):
                ru[i] = ru[i] - l[i][c] * ru[c]
                eu[i] = eu[i] - l[i][c] * eu[c]
        u, w = ru[0], eu[0]
        for c in range(1, 8):
            u = jnp.where(sub == c, ru[c], u)
            w = jnp.where(sub == c, eu[c], w)
        us.append(u)
        ws.append(w)
        for i in range(j + 1, n):
            ri, ei = rows[i], inv_rows[i]
            v = [full(ri[:, 8 * j + c : 8 * j + c + 1]) for c in range(8)]
            for c in range(8):
                v[c] = v[c] * inv[c]
                for d in range(c + 1, 8):
                    v[d] = v[d] - l[d][c] * v[c]
            for c in range(8):
                ri = ri - v[c] * ru[c]
                ei = ei - v[c] * eu[c]
            rows[i], inv_rows[i] = ri, ei
    return jnp.concatenate(us, axis=0), jnp.concatenate(ws, axis=0)

def factor_256(s, lt_ref, w_ref, diag):
    r1 = lax.broadcasted_iota(jnp.int32, (128, 128), 0)
    c1 = lax.broadcasted_iota(jnp.int32, (128, 128), 1)
    right = s[0:128, 128:256]
    diag[0] = s[0:128, 0:128]
    diag[1] = s[128:256, 128:256]
    lt_ref[128:256, 0:128] = jnp.zeros((128, 128), F32)
    w_ref[0:128, 128:256] = jnp.zeros((128, 128), F32)

    @pl.loop(0, 2)
    def _(k):
        at = pl.multiple_of(k * 128, 128)
        u, w = inner(diag[k])
        w = jnp.where(c1 <= r1, w, 0.0)
        lt_ref[pl.ds(at, 128), pl.ds(at, 128)] = jnp.where(c1 >= r1, u, 0.0)
        w_ref[pl.ds(at, 128), pl.ds(at, 128)] = w

        @pl.when(k == 0)
        def _():
            u01 = dot(w, right, 1, 0)
            lt_ref[0:128, 128:256] = u01
            diag[1] -= dot(u01, u01, 0, 0)

    under = dot(lt_ref[0:128, 128:256], w_ref[0:128, 0:128], 0, 0)
    w_ref[128:256, 0:128] = -dot(w_ref[128:256, 128:256], under, 1, 0)


def factor_kernel(d_ref, *rest):
    lt0_ref, lt1_ref, w0_ref, w1_ref, under_ref, s, right, diag = rest
    for j in range(16):
        at = slice(16 * j, 16 * j + 16)
        s[at, :] = d_ref[j, 0]
    factor_256(s, lt0_ref, w0_ref, diag)
    for j in range(16):
        at = slice(16 * j, 16 * j + 16)
        right[at, :] = d_ref[j, 1]
        s[at, :] = d_ref[j, 2]
    u = dot(w0_ref[...], right[...], 1, 0)
    s[...] -= dot(u, u, 0, 0)
    factor_256(s, lt1_ref, w1_ref, diag)
    under_ref[...] = -dot(w1_ref[...], dot(u, w0_ref[...], 0, 0), 1, 0)


def factor(d):
    square = jax.ShapeDtypeStruct((256, 256), F32)
    return pl.pallas_call(
        factor_kernel,
        out_shape=[square] * 5,
        scratch_shapes=[pltpu.VMEM((256, 256), F32)] * 2 + [pltpu.VMEM((2, 128, 128), F32)],
        compiler_params=pltpu.CompilerParams(vmem_limit_bytes=16 * MIB),
        cost_estimate=pl.CostEstimate(flops=0, bytes_accessed=0, transcendentals=0),
    )(d)


def product(a, b):
    return matmul(a[0], b[0]) + (matmul(a[0], b[1]) + matmul(a[1], b[0]))


def columns(is_first, w0_ref, w1_ref, under_ref, mine_ref, other_ref, wt_ref, z_ref):
    w = jnp.concatenate(
        [
            jnp.concatenate([w0_ref[...], jnp.zeros((256, 256), F32)], axis=1),
            jnp.concatenate([under_ref[...], w1_ref[...]], axis=1),
        ],
        axis=0,
    )
    turned = split(w.T)
    wt_ref[0:512, :] = turned[0]
    wt_ref[512:1024, :] = turned[1]
    w = split(w)
    for m in range(4):
        at = slice(256 * m, 256 * m + 256)
        mine, other = mine_ref[m], other_ref[m]
        a0 = jnp.where(is_first, mine, other)
        a1 = jnp.where(is_first, other, mine)
        b0 = product([p[0:256, 0:256] for p in w], split(a0))
        b1 = product([p[256:512] for p in w], split(jnp.concatenate([a0, a1], axis=0)))
        b0, b1 = split(b0), split(b1)
        z0 = product([p[0:256] for p in turned], [jnp.concatenate(p, axis=0) for p in zip(b0, b1)])
        z1 = product([p[256:512, 256:512] for p in turned], b1)
        zh, zl = split(jnp.concatenate([z0, z1], axis=0))
        z_ref[0:512, at] = zh
        z_ref[512:1024, at] = zl
        z_ref[1024:1536, at] = zh


def update_kernel(
    place, x_ref, g_ref, w0_ref, w1_ref, under_ref, lt0_ref, lt1_ref, mine_ref, other_ref, out_ref,
    old, new, tiles, wt, z, old_sem, new_sem, tile_sem,
):
    row, col = place[0], place[1]

    def load(l, mh):
        at = pl.ds(l * 256, 256)
        return pltpu.make_async_copy(
            x_ref.at[at, mh], old.at[l, :, pl.ds(128 * mh, 128)], old_sem.at[l, mh]
        )

    def fetch(l, k):
        return pltpu.make_async_copy(
            g_ref.at[position(row, l, k)], tiles.at[l, k], tile_sem.at[l, k]
        )

    def store(l, mh):
        at = pl.ds(l * 256, 256)
        return pltpu.make_async_copy(
            new.at[l % 2, :, pl.ds(128 * mh, 128)], out_ref.at[at, mh], new_sem.at[l % 2, mh]
        )

    @pl.loop(0, 8)
    def _(l):
        for k in range(2):
            fetch(l, k).start()
        for mh in range(8):
            load(l, mh).start()

    is_first = lax.rem(row, 2) == 0
    columns(is_first, w0_ref, w1_ref, under_ref, mine_ref, other_ref, wt, z)

    @pl.loop(0, 8)
    def _(l):
        for k in range(2):
            fetch(l, k).wait()
        xh, xl = split(jnp.concatenate([tiles[l, 0], tiles[l, 1]], axis=1))
        left = jnp.concatenate([xh, xh, xl], axis=1)

        for mh in range(8):
            load(l, mh).wait()

        @pl.when(l >= 2)
        def _():
            for mh in range(8):
                store(l - 2, mh).wait()

        slot = l % 2
        for m in range(1, 4):
            at = slice(256 * m, 256 * m + 256)
            new[slot, :, at] = old[l, :, at] - matmul(left, z[:, at])

        @pl.when(col > 1)
        def _():
            new[slot, :, 0:256] = old[l, :, 0:256] - matmul(left, z[:, 0:256])

        @pl.when(col == 0)
        def _():
            x = (xh[:, 0:256], xl[:, 0:256])
            new[slot, :, 0:256] = product(x, (wt[0:256, 0:256], wt[512:768, 0:256]))

        @pl.when(col == 1)
        def _():
            new[slot, :, 0:256] = product((xh, xl), (wt[0:512, 256:512], wt[512:1024, 256:512]))

        @pl.when((l == 0) & (row <= 1))
        def _():
            new[slot, :, 256:1024] = jnp.zeros((256, 768), F32)

            @pl.when((row == 0) | (col > 0))
            def _():
                own = jnp.where(row == 0, lt0_ref[...].T, lt1_ref[...].T)
                new[slot, :, 0:256] = jnp.where(col == row, own, 0.0)

        for mh in range(8):
            store(l, mh).start()

    for l in (6, 7):
        for mh in range(8):
            store(l, mh).wait()


def position(row, l, k):
    q = 2 * (l // 2) + k
    x = (row // 4 + 2 * (l % 2) + q // 4) % 4
    y = (row % 4 + q % 4) % 4
    return 4 * x + y


def update(place, x, gathered, w0, w1, under, lt0, lt1, mine, other):
    vmem = pl.BlockSpec(memory_space=pltpu.VMEM)
    hbm = pl.BlockSpec(memory_space=pl.ANY)
    return pl.pallas_call(
        update_kernel,
        in_specs=[pl.BlockSpec(memory_space=pltpu.SMEM), hbm, hbm] + [vmem] * 7,
        out_specs=hbm,
        out_shape=jax.ShapeDtypeStruct((2048, 8, 128), F32),
        scratch_shapes=[
            pltpu.VMEM((8, 256, 1024), F32),
            pltpu.VMEM((2, 256, 1024), F32),
            pltpu.VMEM((8, 2, 256, 256), F32),
            pltpu.VMEM((1024, 512), BF16),
            pltpu.VMEM((1536, 1024), BF16),
            pltpu.SemaphoreType.DMA((8, 8)),
            pltpu.SemaphoreType.DMA((2, 8)),
            pltpu.SemaphoreType.DMA((8, 2)),
        ],
        compiler_params=pltpu.CompilerParams(vmem_limit_bytes=48 * MIB),
    )(place, x, gathered, w0, w1, under, lt0, lt1, mine, other)


def scatter_pairs(m):
    pairs = []
    for k in range(2):
        for c in range(COLS):
            row = c % ROWS
            target = position(row, 2 * m + c // ROWS, k)
            pairs.append((k * COLS + c, row * COLS + target))
    return pairs


def along_z(array, step):
    return lax.ppermute(array, "row", [(k, 2 * step + k) for k in range(2)])


def shards(kernel):
    row, col = lax.axis_index("row"), lax.axis_index("col")
    place = jnp.stack([row, col]).astype(jnp.int32)
    x = kernel.reshape(16384, 128)
    tile, tiles, *turned = prepare(x)

    pieces = [lax.ppermute(turned[m], ("row", "col"), scatter_pairs(m)) for m in range(4)]
    d = lax.all_to_all(tile.reshape(16, 16, 256), "col", 0, 0, tiled=True)[0:2]
    pieces, d = lax.optimization_barrier((pieces, d))
    share = sum(pieces)
    share, d = lax.optimization_barrier((share, d))
    gathered = lax.all_gather(share, "col")

    d = lax.all_to_all(jnp.broadcast_to(d[None], (8, 2, 16, 256)), "row", 0, 0, tiled=True)
    d = jnp.stack([d[0, 0], d[0, 1], d[1, 1]])
    tiles, d = lax.optimization_barrier((tiles, d))
    came = [along_z(tiles, step) for step in (1, 3, 2)]
    d = lax.all_to_all(jnp.broadcast_to(d[None], (16, 3, 16, 256)), "col", 0, 0, tiled=True)
    lt0, lt1, w0, w1, under = factor(d)

    came, w1 = lax.optimization_barrier((came, w1))
    mine = jnp.where(row < 2, tiles, sum(came))
    other = lax.ppermute(mine, "row", [(r, r ^ 1) for r in range(ROWS)])
    cells = kernel.reshape(2048, 8, 128)
    out = update(place, cells, gathered, w0, w1, under, lt0, lt1, mine, other)
    return out.reshape(kernel.shape)


def solution(mesh):
    placed = P(None, "row", None, None, "col", None)
    return jax.shard_map(
        shards, mesh=mesh, in_specs=(placed,), out_specs=placed, check_vma=False
    )
```
